128 devices in a mesh: blk: 16 (over z_hi, x, core), tp: 8 (over y, z_lo).
Axes of the slice: x: 4, y: 4, z: 4 (z_hi: 2, z_lo: 2; z = z_hi * 2 + z_lo), core: 2. Of those that a mesh axis runs over, the one named last changes fastest.
Arguments:
- act_rows: bfloat16 [8, 128, 524288], P('tp', None, 'blk'), may hold values from -6 to 6
- grad_rows: bfloat16 [8, 64, 524288], P('tp', None, 'blk'), may hold values from -0.59765625 to 0.59765625
- query_grads: bfloat16 [256, 8, 64, 128], P('blk', 'tp'), may hold values from -0.0234375 to 0.0234375
- ginv: float32 [8, 64, 64], P('tp'), as said below
- ainv: float32 [8, 128, 128], P('tp'), as said below
- lengths: int32 [128, 64], P(('blk', 'tp')), may hold values from 1 to 128, 4096 in all within a row
Outputs:
- scores: float32 [8192, 256], P(('blk', 'tp'))
The draws below stay inside these ranges and needn't reach their ends.
Inputs may be any that keep to these rules, and one draw needn't show every extreme that they name: `lengths`: each row sums to 4096, and each row's largest entry is 128. `ginv`: Symmetric. `ainv`: Symmetric.
All inputs are finite; a program needn't handle non-finite values.
Results may differ from the reference program's by a relative error of at most 0.0041.
Values may be sent and summed in bfloat16 or wider, within the bound.
No kernel may reach another device: no remote copies, remote signals or barrier semaphores. Data moves between devices by JAX's collectives and lax.ppermute only.
A program may use at most 128 MiB of HBM per device.

```python
import math
import jax
import jax.numpy as jnp
import numpy as np
from jax import lax

KA = 128
KG = 64
DDEV = 64
MOST = 128
TOK_DEV = 4096
LAYERS = 8
DOCS = 8192
QUERIES = 256
TOKENS = 524288
N_BLK = 16
N_TP = 8


def factor_matrix(diag_key, noise, size):
    diagonal = jax.random.uniform(diag_key, noise.shape[:2], jnp.float32, 1.0, 2.0)
    symmetric = noise + jnp.swapaxes(noise, 1, 2)
    return jnp.eye(size, dtype=jnp.float32)[None] * diagonal[:, :, None] + 0.3 / math.sqrt(size) * symmetric


def draw_ginv(key, part):
    key = jax.random.fold_in(key, 11)
    diag_key, off_key = jax.random.split(key)
    noise = jax.random.normal(off_key, (LAYERS, KG, KG), jnp.float32)
    return factor_matrix(diag_key, noise, KG)


def draw_ainv(key, part):
    key = jax.random.fold_in(key, 23)
    diag_key, off_key = jax.random.split(key)
    noise = jax.random.normal(off_key, (LAYERS, KA, KA), jnp.float32)
    return factor_matrix(diag_key, noise, KA)


def levels(stream_key, shape, pieces, low, largest):
    factor_of, own = 1.0, jax.random.fold_in(stream_key, 6)
    for position, parts in pieces:
        steps = jnp.exp(jax.random.uniform(jax.random.fold_in(own, position), (parts,), jnp.float32, low / len(pieces), largest / len(pieces)))
        factor_of = factor_of * jnp.repeat(steps, shape[position] // parts).reshape([-1 if axis == position else 1 for axis in range(len(shape))])
    return factor_of


def profile(number_of, total, most, lean):
    weights = [(1 << 20) // math.isqrt(rank ** lean) + 1 for rank in range(2, number_of + 1)]
    surplus, holding = total - most - (number_of - 1), [1] * (number_of - 1)
    while surplus > 0:
        free = [i for i in range(number_of - 1) if holding[i] < most]
        whole, left = sum([weights[i] for i in free]), surplus
        for i in free:
            more = min(most - holding[i], max(1, left * weights[i] // whole), surplus)
            holding[i] = holding[i] + more
            surplus = surplus - more
    return np.array([most] + holding)


def ragged(key, number_of, total, most, skew):
    if number_of == 2:
        one = jax.random.randint(key, (), max(1, total - most), min(most, total - 1) + 1)
        return jnp.stack([one, total - one])
    sizes = jnp.asarray(profile(number_of, total, most, skew), jnp.int32)
    pairs = (number_of - 1) // 2
    source_of, receiver = sizes[1:1 + 2 * pairs:2], sizes[2:2 + 2 * pairs:2]
    margin = jnp.minimum(source_of - 1, most - receiver)
    moved = jax.random.randint(jax.random.fold_in(key, 1), (pairs,), 0, 1 << 20) % (margin + 1)
    sizes = sizes.at[1:1 + 2 * pairs:2].set(source_of - moved).at[2:2 + 2 * pairs:2].set(receiver + moved)
    return sizes[jax.random.permutation(jax.random.fold_in(key, 2), number_of)]


def gaussian(key, shape, width, reach, cuts=(), kind=jnp.bfloat16):
    array = jax.random.normal(key, shape, jnp.float32) * width
    if len(cuts) > 0:
        array = levels(key, shape, cuts, -0.22, 0.18) * array
    return jnp.clip(array, min=-reach, max=reach).astype(kind)


def setup_inputs(seed: int = 0) -> dict:
    arg_keys = jax.random.split(jax.random.key(seed), 7)
    act_rows = gaussian(arg_keys[0], (LAYERS, KA, TOKENS), 1.0, 6.0, ((0, 8), (2, 16)))
    grad_rows = gaussian(arg_keys[1], (LAYERS, KG, TOKENS), 0.1, 0.59765625, ((0, 8), (2, 16)))
    query_grads = gaussian(arg_keys[2], (QUERIES, LAYERS, KG, KA), (LAYERS * KG * KA) ** -0.5, 0.0234375, ((0, 16), (1, 8)))
    ginv = draw_ginv(jax.random.fold_in(arg_keys[6], 71), 0)
    ainv = draw_ainv(jax.random.fold_in(arg_keys[6], 71), 0)
    lengths = jax.vmap(lambda own: ragged(own, DDEV, TOK_DEV, MOST, 2))(jax.random.split(arg_keys[5], (N_BLK * N_TP))).reshape((N_BLK * N_TP, DDEV)).astype(jnp.int32)
    return dict(act_rows=act_rows, grad_rows=grad_rows, query_grads=query_grads, ginv=ginv, ainv=ainv, lengths=lengths)


def doc_gradients(activations, gradients, doc_lengths):
    owner_rows = doc_lengths.shape[0]
    per_owner = activations.shape[2] // owner_rows
    bases = (jnp.arange(owner_rows, dtype=jnp.int32) * per_owner)[:, None]
    starts = (jnp.cumsum(doc_lengths, axis=1) - doc_lengths + bases).reshape(-1).astype(jnp.int32)
    flat_lengths = doc_lengths.reshape(-1)
    offsets_in = jnp.arange(MOST, dtype=jnp.int32)
    token_index = jnp.minimum(starts[:, None] + offsets_in[None, :], activations.shape[2] - 1).astype(jnp.int32)
    inside = (offsets_in[None, :] < flat_lengths[:, None]).astype(activations.dtype)
    picked_acts = jnp.take(activations, token_index, axis=2) * inside
    picked_grads = jnp.take(gradients, token_index, axis=2)
    outer_sums = jnp.einsum('lgdm,ladm->dlga', picked_grads.astype(jnp.float32), picked_acts.astype(jnp.float32))
    return outer_sums.astype(jnp.bfloat16).reshape(outer_sums.shape[0], -1)


def precondition(query_grads, ginv, ainv):
    left_side = jnp.einsum('lgh,qlha->qlga', ginv, query_grads.astype(jnp.float32), precision=lax.Precision.HIGHEST)
    both_sides = jnp.einsum('qlga,lab->qlgb', left_side, ainv, precision=lax.Precision.HIGHEST)
    return both_sides.astype(jnp.bfloat16)


def reference(act_rows, grad_rows, query_grads, ginv, ainv, lengths):
    query_panel = precondition(query_grads, ginv, ainv).reshape(QUERIES, -1)

    def owner_tile(owner_id):
        start = (owner_id * TOK_DEV).astype(jnp.int32)
        activations = lax.dynamic_slice_in_dim(act_rows, start, TOK_DEV, 2)
        gradients = lax.dynamic_slice_in_dim(grad_rows, start, TOK_DEV, 2)
        doc_lengths = lax.dynamic_slice_in_dim(lengths, owner_id.astype(jnp.int32), 1, 0)
        documents = doc_gradients(activations, gradients, doc_lengths)
        return jnp.dot(documents, query_panel.T, preferred_element_type=jnp.float32)

    tiles = lax.map(owner_tile, jnp.arange(N_BLK * N_TP, dtype=jnp.int32))
    return tiles.reshape(DOCS, QUERIES)
```

```python
import functools

import jax
import jax.numpy as jnp
from jax import lax
from jax.experimental import pallas as pl
from jax.experimental.pallas import tpu as pltpu
from jax.sharding import PartitionSpec as P

F32, BF16 = jnp.float32, jnp.bfloat16
KA, KG, DOCS, TOK = 128, 64, 64, 4096
WIDTH = KA * KG
HALF = WIDTH // 2
ORDER = (0, 1, 2, 3, 6, 7, 4, 5)
NT = (((1,), (1,)), ((), ()))
DOC_PITCH = 72
QUERY_PITCH = 24


def from_partner(block, axis, mask):
    n = lax.axis_size(axis)
    return lax.ppermute(block, axis, [(i ^ mask, i) for i in range(n)])


def bf16_parts(x):
    first = x.astype(BF16)
    rest = x - first.astype(F32)
    second = rest.astype(BF16)
    third = (rest - second.astype(F32)).astype(BF16)
    return first, second, third


def panel_kernel(query_ref, ginv_ref, ainv_ref, out_ref, rows):
    count = query_ref.shape[0]
    queries = query_ref[...].reshape(count * KG, KA)
    right = sum(
        jnp.dot(queries, part, preferred_element_type=F32)
        for part in reversed(bf16_parts(ainv_ref[0]))
    )
    side_by_side = jnp.concatenate(
        [right[q * KG : (q + 1) * KG] for q in range(count)], axis=1
    )
    both = jnp.dot(
        ginv_ref[0], side_by_side, precision=lax.Precision.HIGHEST, preferred_element_type=F32
    )
    for q in range(count):
        rows[pl.ds(q, KG, stride=QUERY_PITCH), :] = both[:, q * KA : (q + 1) * KA]
    for g in range(KG):
        out_ref[:, g * KA : (g + 1) * KA] = rows[pl.ds(g * QUERY_PITCH, count), :].astype(BF16)


def panel(query_grads, ginv, ainv):
    count = query_grads.shape[0]
    return pl.pallas_call(
        panel_kernel,
        out_shape=jax.ShapeDtypeStruct((count, WIDTH), BF16),
        scratch_shapes=[pltpu.VMEM((KG * QUERY_PITCH, KA), F32)],
        compiler_params=pltpu.CompilerParams(vmem_limit_bytes=32 << 20),
        cost_estimate=pl.CostEstimate(flops=400_000_000, bytes_accessed=1 << 20, transcendentals=0),
        name="panel",
    )(query_grads.reshape(count, KG, KA), ginv, ainv)


def docs_kernel(at_ref, lengths_ref, act_ref, grad_ref, out_ref, rows):
    o = pl.program_id(0)
    lane = lax.broadcasted_iota(jnp.int32, (KG, 256), 1)

    def document(j, start):
        end = start + lengths_ref[o, j]
        base = pl.multiple_of(jnp.minimum(start >> 7, TOK // 128 - 2) * 128, 128)
        acts = act_ref[0, :, pl.ds(base, 256)]
        grads = grad_ref[0, :, pl.ds(base, 256)]
        inside = (lane >= start - base) & (lane < end - base)
        grads = jnp.where(inside, grads, jnp.zeros_like(grads))
        rows[pl.ds(j, KG, stride=DOC_PITCH), :] = lax.dot_general(
            grads, acts, NT, preferred_element_type=F32
        )
        return end

    lax.fori_loop(0, DOCS, document, jnp.int32(0), unroll=32)
    for g in range(KG):
        out_ref[:, g * KA : (g + 1) * KA] = rows[pl.ds(g * DOC_PITCH, DOCS), :].astype(BF16)


def doc_gradients(owner_at, lengths, act_rows, grad_rows):
    owners = lengths.shape[0]
    return pl.pallas_call(
        docs_kernel,
        grid_spec=pltpu.PrefetchScalarGridSpec(
            num_scalar_prefetch=2,
            grid=(owners,),
            in_specs=[
                pl.BlockSpec((1, KA, TOK), lambda o, at, n: (0, 0, at[o])),
                pl.BlockSpec((1, KG, TOK), lambda o, at, n: (0, 0, at[o])),
            ],
            out_specs=pl.BlockSpec((DOCS, WIDTH), lambda o, at, n: (o, 0)),
            scratch_shapes=[pltpu.VMEM((KG * DOC_PITCH, KA), F32)],
        ),
        out_shape=jax.ShapeDtypeStruct((owners * DOCS, WIDTH), BF16),
        compiler_params=pltpu.CompilerParams(vmem_limit_bytes=32 << 20),
        cost_estimate=pl.CostEstimate(
            flops=owners * 2_000_000_000, bytes_accessed=owners * 5 << 19, transcendentals=0
        ),
        name="docs",
    )(owner_at, lengths, act_rows, grad_rows)


K_BLOCK = 1024


def score_kernel(doc_ref, *refs):
    k = pl.program_id(0)
    *piece_refs, out_ref = refs
    pieces = [ref[...] for ref in piece_refs]
    halves = pieces[12:]
    low = k < HALF // K_BLOCK
    whole = pieces[:12] + [
        jnp.where(low, halves[2 * i], halves[2 * i + 1]) for i in range(len(halves) // 2)
    ]
    by_mask = dict(zip(WHOLE + SPLIT, whole))
    panels = jnp.concatenate([by_mask[m] for m in range(16)], axis=0)
    tile = lax.dot_general(doc_ref[...], panels, NT, preferred_element_type=F32)

    @pl.when(k == 0)
    def _():
        out_ref[...] = tile

    @pl.when(k > 0)
    def _():
        out_ref[...] += tile


WHOLE = (0, 2, 6, 8, 10, 14, 1, 3, 7, 9, 11, 15)
SPLIT = (4, 12, 5, 13)


def partial_scores(documents, whole, split):
    rows, count = documents.shape[0], whole[0].shape[0]
    half_steps = HALF // K_BLOCK
    in_specs = [pl.BlockSpec((rows, K_BLOCK), lambda k: (0, k))]
    in_specs += [pl.BlockSpec((count, K_BLOCK), lambda k: (0, k)) for _ in whole]
    flat = []
    for low, high in split:
        in_specs.append(pl.BlockSpec((count, K_BLOCK), lambda k: (0, jnp.minimum(k, half_steps - 1))))
        in_specs.append(pl.BlockSpec((count, K_BLOCK), lambda k: (0, jnp.maximum(k - half_steps, 0))))
        flat += [low, high]
    return pl.pallas_call(
        score_kernel,
        grid=(WIDTH // K_BLOCK,),
        in_specs=in_specs,
        out_specs=pl.BlockSpec((rows, 16 * count), lambda k: (0, 0)),
        out_shape=jax.ShapeDtypeStruct((rows, 16 * count), F32),
        compiler_params=pltpu.CompilerParams(vmem_limit_bytes=32 << 20),
        cost_estimate=pl.CostEstimate(
            flops=2 * rows * 16 * count * WIDTH, bytes_accessed=12 << 20, transcendentals=0
        ),
        name="scores",
    )(documents, *whole, *flat)


def place_kernel(blk_ref, mine_ref, theirs_ref, out_ref):
    x = mine_ref[...] + theirs_ref[...]
    lane = lax.broadcasted_iota(jnp.int32, x.shape, 1)
    width = x.shape[1]
    for bit in range(4):
        step = width // 16 << bit
        swapped = jnp.where(
            lane & step != 0, pltpu.roll(x, step, 1), pltpu.roll(x, width - step, 1)
        )
        x = jnp.where((blk_ref[0] >> bit) & 1 != 0, swapped, x)
    out_ref[...] = x


def place(blk, mine, theirs):
    vmem = pl.BlockSpec(memory_space=pltpu.VMEM)
    return pl.pallas_call(
        place_kernel,
        in_specs=[pl.BlockSpec(memory_space=pltpu.SMEM), vmem, vmem],
        out_specs=vmem,
        out_shape=jax.ShapeDtypeStruct(mine.shape, F32),
        name="place",
    )(blk, mine, theirs)


def local(act_rows, grad_rows, query_grads, ginv, ainv, lengths):
    blk, tp = lax.axis_index("blk"), lax.axis_index("tp")

    for mask in (1, 2, 6):
        lengths = jnp.concatenate([lengths, from_partner(lengths, "tp", mask)], axis=0)
    owner_at = jnp.int32(tp) ^ jnp.asarray(ORDER, jnp.int32)

    own = panel(query_grads, ginv, ainv)

    def take(block, mask):
        return from_partner(block, "blk", mask)

    got, halves = {0: own}, {}
    got[8] = take(own, 8)
    got[2], got[6] = take(own, 2), take(own, 6)
    for z in (0, 8):
        if z:
            got[z | 2], got[z | 6] = take(got[z], 2), take(got[z], 6)
        halves[z | 4] = (
            take(got[z | 6][:, :HALF], 2),
            take(got[z | 2][:, HALF:], 6),
        )
    for mask in list(got):
        got[mask | 1] = take(got[mask], 1)
    for mask in list(halves):
        halves[mask | 1] = tuple(take(part, 1) for part in halves[mask])

    documents = doc_gradients(owner_at, lengths, act_rows, grad_rows)
    scores = partial_scores(documents, [got[m] for m in WHOLE], [halves[m] for m in SPLIT])

    for mask in (6, 2):
        rows = scores.shape[0] // 2
        scores = scores[:rows] + from_partner(scores[rows:], "tp", mask)
    rows = scores.shape[0] // 2
    theirs = from_partner(scores[rows:], "tp", 1)
    return place(jnp.int32(blk).reshape(1), scores[:rows], theirs)


def solution(mesh):
    placed = (
        P("tp", None, "blk"),
        P("tp", None, "blk"),
        P("blk", "tp", None, None),
        P("tp", None, None),
        P("tp", None, None),
        P(("blk", "tp"), None),
    )
    return jax.shard_map(
        local, mesh=mesh, in_specs=placed, out_specs=P(("blk", "tp"), None), check_vma=False
    )
```

```python
import functools

import jax
import jax.numpy as jnp
from jax import lax
from jax.experimental import pallas as pl
from jax.experimental.pallas import tpu as pltpu
from jax.sharding import PartitionSpec as P

F32, BF16 = jnp.float32, jnp.bfloat16
KA, KG, DOCS, TOK = 128, 64, 64, 4096
WIDTH = KA * KG
HALF = WIDTH // 2
NT = (((1,), (1,)), ((), ()))
OWNERS = 8
CALL = 4
PITCH = CALL * DOCS + 8
STEPS = 38
QUERY_PITCH = 24

HBM = pl.BlockSpec(memory_space=pltpu.MemorySpace.HBM)
ANY = pl.BlockSpec(memory_space=pl.ANY)
VMEM = pl.BlockSpec(memory_space=pltpu.VMEM)
SMEM = pl.BlockSpec(memory_space=pltpu.SMEM)


def in_hbm(x):
    return pltpu.with_memory_space_constraint(x, pltpu.HBM)


def in_vmem(x):
    return pltpu.with_memory_space_constraint(x, pltpu.VMEM)


def from_partner(block, axis, mask):
    n = lax.axis_size(axis)
    return lax.ppermute(block, axis, [(i ^ mask, i) for i in range(n)])


def bf16_parts(x):
    first = x.astype(BF16)
    rest = x - first.astype(F32)
    second = rest.astype(BF16)
    third = (rest - second.astype(F32)).astype(BF16)
    return first, second, third


def panel_kernel(
    query_hbm, ginv_hbm, ainv_hbm, lengths_hbm, out_ref, lengths_ref, query_ref, ginv_ref, ainv_ref, rows, sem
):
    count = query_ref.shape[0]
    loads = [
        pltpu.make_async_copy(ainv_hbm.at[0], ainv_ref, sem.at[0]),
        pltpu.make_async_copy(query_hbm, query_ref, sem.at[1]),
        pltpu.make_async_copy(ginv_hbm.at[0], ginv_ref, sem.at[2]),
        pltpu.make_async_copy(lengths_hbm, lengths_ref, sem.at[3]),
    ]
    for load in loads:
        load.start()
    for load in loads:
        load.wait()
    queries = query_ref[...].reshape(count * KG, KA)
    right = sum(
        jnp.dot(queries, part, preferred_element_type=F32)
        for part in reversed(bf16_parts(ainv_ref[...]))
    )
    side_by_side = jnp.concatenate(
        [right[q * KG : (q + 1) * KG] for q in range(count)], axis=1
    )
    both = jnp.dot(
        ginv_ref[...], side_by_side, precision=lax.Precision.HIGHEST, preferred_element_type=F32
    )
    for q in range(count):
        rows[pl.ds(q, KG, stride=QUERY_PITCH), :] = both[:, q * KA : (q + 1) * KA]
    for g in range(KG):
        out_ref[:, g * KA : (g + 1) * KA] = rows[pl.ds(g * QUERY_PITCH, count), :].astype(BF16)


def panel(query_grads, ginv, ainv, lengths):
    count = query_grads.shape[0]
    return pl.pallas_call(
        panel_kernel,
        in_specs=[HBM] * 4,
        out_specs=[VMEM, VMEM],
        out_shape=[pltpu.VMEM((count, WIDTH), BF16), pltpu.VMEM(lengths.shape, lengths.dtype)],
        scratch_shapes=[
            pltpu.VMEM((count, KG, KA), BF16),
            pltpu.VMEM((KG, KG), F32),
            pltpu.VMEM((KA, KA), F32),
            pltpu.VMEM((KG * QUERY_PITCH, KA), F32),
            pltpu.SemaphoreType.DMA((4,)),
        ],
        compiler_params=pltpu.CompilerParams(vmem_limit_bytes=8 << 20),
        cost_estimate=pl.CostEstimate(flops=400_000_000, bytes_accessed=1 << 20, transcendentals=0),
        name="panel",
    )(
        in_hbm(query_grads.reshape(count, KG, KA)),
        in_hbm(ginv),
        in_hbm(ainv),
        in_hbm(lengths),
    )


def docs_kernel(first, tp_ref, lengths_ref, act_hbm, grad_hbm, *refs):
    out_ref, act_ref, grad_ref, sem = refs[-4:]
    tp = tp_ref[0]
    lane = lax.broadcasted_iota(jnp.int32, (1, 256), 1)

    def loads(o):
        tokens = pl.ds(pl.multiple_of((first + o) * TOK, TOK), TOK)
        return (
            pltpu.make_async_copy(act_hbm.at[0, :, tokens], act_ref.at[o], sem.at[0, o]),
            pltpu.make_async_copy(grad_hbm.at[0, :, tokens], grad_ref.at[o], sem.at[1, o]),
        )

    for o in range(CALL):
        for load in loads(o):
            load.start()

    def owner(o, _):
        for load in loads(o):
            load.wait()
        row = first + o
        acts, grads = act_ref.at[o], grad_ref.at[o]

        def product(carry):
            j, start = carry
            base = pl.multiple_of(jnp.minimum(start >> 7, TOK // 128 - 2) * 128, 128)
            middle = start + lengths_ref[row, jnp.minimum(j, DOCS - 1)]
            end = middle + lengths_ref[row, jnp.minimum(j + 1, DOCS - 1)]
            window = grads[:, pl.ds(base, 256)]
            at = lane + base
            one = jnp.where((at >= start) & (at < middle), 1.0, 0.0).astype(BF16)
            two = jnp.where((at >= middle) & (at < end), 1.0, 0.0).astype(BF16)
            pair = lax.dot_general(
                jnp.concatenate([window * one, window * two], axis=0),
                acts[:, pl.ds(base, 256)],
                NT,
                preferred_element_type=F32,
            )
            out_ref[pl.ds(o * DOCS + j, KG, stride=PITCH), :] = pair[:KG]
            out_ref[pl.ds(o * DOCS + j + 1, KG, stride=PITCH), :] = pair[KG:]
            fits = end <= base + 256
            return (
                jnp.minimum(jnp.where(fits, j + 2, j + 1), DOCS),
                jnp.where(fits, end, middle),
            )

        carry = (jnp.int32(0), jnp.int32(0))
        for _ in range(STEPS):
            carry = product(carry)
        lax.while_loop(lambda c: c[0] < DOCS, lambda c: product(product(c)), carry)
        return 0

    lax.fori_loop(0, CALL, owner, 0)


def doc_gradients(first, tp, lengths, act_rows, grad_rows, after):
    return pl.pallas_call(
        functools.partial(docs_kernel, first),
        in_specs=[SMEM, SMEM, HBM, HBM] + [ANY] * len(after),
        out_specs=VMEM,
        out_shape=pltpu.VMEM((KG * PITCH, KA), F32),
        scratch_shapes=[
            pltpu.VMEM((CALL, KA, TOK), BF16),
            pltpu.VMEM((CALL, KG, TOK), BF16),
            pltpu.SemaphoreType.DMA((2, CALL)),
        ],
        compiler_params=pltpu.CompilerParams(vmem_limit_bytes=10 << 20),
        cost_estimate=pl.CostEstimate(
            flops=CALL * 2_000_000_000, bytes_accessed=CALL * 5 << 19, transcendentals=0
        ),
        name="docs",
    )(tp, lengths, in_hbm(act_rows), in_hbm(grad_rows), *after)


K_STEP = 1024


def group_kernel(*refs, halves):
    count, out_ref = refs[-2].shape[0], refs[-1]
    if halves:
        out_ref[:count, :HALF] = refs[0][...]
        out_ref[:count, HALF:] = refs[1][...]
    for i, ref in enumerate(refs[2:5] if halves else refs[:4]):
        out_ref[pl.ds((i + halves) * count, count), :] = ref[...]


def group(pieces, after):
    halves = pieces[0].shape[1] == HALF
    count = pieces[-1].shape[0]

    def kernel(*refs):
        group_kernel(*refs[len(after) :], halves=halves)

    return pl.pallas_call(
        kernel,
        in_specs=[ANY] * len(after) + [VMEM] * len(pieces),
        out_specs=VMEM,
        out_shape=pltpu.VMEM((4 * count, WIDTH), BF16),
        compiler_params=pltpu.CompilerParams(vmem_limit_bytes=4 << 20),
        cost_estimate=pl.CostEstimate(flops=0, bytes_accessed=1 << 20, transcendentals=0),
        name="group",
    )(*after, *pieces)


NEAR = (0, 2, 6, 8)
FAR = (4, 10, 14, 12)


def score_kernel(group_masks, blk_ref, *refs):
    *group_refs, out_ref, panels, total = refs
    docs_refs, group_refs = group_refs[:2], group_refs[2:]
    count, rows = panels.shape[0] // 16, total.shape[0]
    for masks, group in zip(group_masks, group_refs):
        for i, m in enumerate(masks):
            panels[pl.ds(pl.multiple_of((blk_ref[0] ^ m) * count, count), count), :] = group[
                i * count : (i + 1) * count, :
            ]
    for half, docs_ref in enumerate(docs_refs):
        for k in range(0, WIDTH, K_STEP):
            documents = jnp.concatenate(
                [
                    docs_ref[pl.ds((k // KA + i) * PITCH, rows), :].astype(BF16)
                    for i in range(K_STEP // KA)
                ],
                axis=1,
            )
            tile = lax.dot_general(
                documents, panels[:, k : k + K_STEP], NT, preferred_element_type=F32
            )
            if k == 0:
                total[...] = tile
            elif k < WIDTH - K_STEP:
                total[...] += tile
            else:
                tile = (total[...] + tile).astype(BF16).reshape(CALL, DOCS, tile.shape[1])
                out_ref[pl.ds(half * CALL, CALL)] = tile


def partial_scores(blk, documents, group_masks, groups):
    count = sum(group.shape[0] for group in groups)
    return pl.pallas_call(
        functools.partial(score_kernel, group_masks),
        in_specs=[SMEM] + [VMEM] * (len(documents) + len(groups)),
        out_specs=VMEM,
        out_shape=pltpu.VMEM((OWNERS, DOCS, count), BF16),
        scratch_shapes=[
            pltpu.VMEM((count, WIDTH), BF16),
            pltpu.VMEM((CALL * DOCS, count), F32),
        ],
        compiler_params=pltpu.CompilerParams(vmem_limit_bytes=10 << 20),
        cost_estimate=pl.CostEstimate(
            flops=2 * OWNERS * DOCS * count * WIDTH, bytes_accessed=12 << 20, transcendentals=0
        ),
        name="scores",
    )(blk, *map(in_vmem, documents), *map(in_vmem, groups))


def local(act_rows, grad_rows, query_grads, ginv, ainv, lengths):
    blk = lax.axis_index("blk").astype(jnp.int32).reshape(1)
    tp = lax.axis_index("tp").astype(jnp.int32).reshape(1)

    def take(block, mask):
        return from_partner(block, "blk", mask)

    own, lengths = panel(query_grads, ginv, ainv, lengths)
    got = {0: own}
    for mask in (6, 2, 8, 12):
        got[mask] = take(own, mask)

    lengths = lax.all_to_all(
        jnp.broadcast_to(lengths, (OWNERS, DOCS)), "tp", split_axis=0, concat_axis=0, tiled=True
    )

    near = group([got[m] for m in NEAR], [lengths])
    near_other = take(near, 1)
    count = own.shape[0]
    sent = {m: near[i * count : (i + 1) * count] for i, m in enumerate(NEAR)}
    got[4] = [take(sent[6][:, :HALF], 2), take(sent[2][:, HALF:], 6)]
    got[10], got[14] = take(sent[8], 2), take(sent[8], 6)

    low = doc_gradients(0, tp, lengths, act_rows, grad_rows, [near_other])
    far = group([*got[4], got[10], got[14], got[12]], [low])
    far_other = [take(far[i * count : (i + 1) * count], 1) for i in range(4)]
    high = doc_gradients(CALL, tp, lengths, act_rows, grad_rows, [far])

    parts = partial_scores(
        blk,
        [low, high],
        [NEAR, [m ^ 1 for m in NEAR], FAR] + [[m ^ 1] for m in FAR],
        [near, near_other, far, *far_other],
    )
    parts = lax.all_to_all(parts, "tp", split_axis=0, concat_axis=0)
    return jnp.sum(parts.astype(F32), axis=0)


def solution(mesh):
    placed = (
        P("tp", None, "blk"),
        P("tp", None, "blk"),
        P("blk", "tp", None, None),
        P("tp", None, None),
        P("tp", None, None),
        P(("blk", "tp"), None),
    )
    return jax.shard_map(
        local, mesh=mesh, in_specs=placed, out_specs=P(("blk", "tp"), None), check_vma=False
    )
```

```python
import functools

import jax
import jax.numpy as jnp
from jax import lax
from jax.experimental import pallas as pl
from jax.experimental.pallas import tpu as pltpu
from jax.sharding import PartitionSpec as P

F32, BF16 = jnp.float32, jnp.bfloat16
KA, KG, DOCS, TOK = 128, 64, 64, 4096
WIDTH = KA * KG
HALF = WIDTH // 2
NT = (((1,), (1,)), ((), ()))
OWNERS = 8
CALLS = (6, 2)
STEPS = 38
QUERY_PITCH = 24


def doc_pitch(owners):
    return owners * DOCS + 8


HBM = pl.BlockSpec(memory_space=pltpu.MemorySpace.HBM)
ANY = pl.BlockSpec(memory_space=pl.ANY)
VMEM = pl.BlockSpec(memory_space=pltpu.VMEM)
SMEM = pl.BlockSpec(memory_space=pltpu.SMEM)


def in_hbm(x):
    return pltpu.with_memory_space_constraint(x, pltpu.HBM)


def in_vmem(x):
    return pltpu.with_memory_space_constraint(x, pltpu.VMEM)


def from_partner(block, axis, mask):
    n = lax.axis_size(axis)
    return lax.ppermute(block, axis, [(i ^ mask, i) for i in range(n)])


def bf16_parts(x):
    first = x.astype(BF16)
    rest = x - first.astype(F32)
    second = rest.astype(BF16)
    third = (rest - second.astype(F32)).astype(BF16)
    return first, second, third


def panel_kernel(
    query_hbm, ginv_hbm, ainv_hbm, lengths_hbm,
    out_ref, lengths_ref,
    query_ref, ginv_ref, ainv_ref, rows, sem,
):
    count = query_ref.shape[0]
    loads = [
        pltpu.make_async_copy(ainv_hbm.at[0], ainv_ref, sem.at[0]),
        pltpu.make_async_copy(query_hbm, query_ref, sem.at[1]),
        pltpu.make_async_copy(ginv_hbm.at[0], ginv_ref, sem.at[2]),
        pltpu.make_async_copy(lengths_hbm, lengths_ref, sem.at[3]),
    ]
    for load in loads:
        load.start()
    for load in loads:
        load.wait()
    queries = query_ref[...].reshape(count * KG, KA)
    right = sum(
        jnp.dot(queries, part, preferred_element_type=F32)
        for part in reversed(bf16_parts(ainv_ref[...]))
    )
    side_by_side = jnp.concatenate(
        [right[q * KG : (q + 1) * KG] for q in range(count)], axis=1
    )
    both = jnp.dot(
        ginv_ref[...], side_by_side, precision=lax.Precision.HIGHEST, preferred_element_type=F32
    )
    for q in range(count):
        rows[pl.ds(q, KG, stride=QUERY_PITCH), :] = both[:, q * KA : (q + 1) * KA]
    for g in range(KG):
        out_ref[:, g * KA : (g + 1) * KA] = rows[pl.ds(g * QUERY_PITCH, count), :].astype(BF16)


def panel(query_grads, ginv, ainv, lengths):
    count = query_grads.shape[0]
    return pl.pallas_call(
        panel_kernel,
        in_specs=[HBM] * 4,
        out_specs=[VMEM, VMEM],
        out_shape=[pltpu.VMEM((count, WIDTH), BF16), pltpu.VMEM(lengths.shape, lengths.dtype)],
        scratch_shapes=[
            pltpu.VMEM((count, KG, KA), BF16),
            pltpu.VMEM((KG, KG), F32),
            pltpu.VMEM((KA, KA), F32),
            pltpu.VMEM((KG * QUERY_PITCH, KA), F32),
            pltpu.SemaphoreType.DMA((4,)),
        ],
        compiler_params=pltpu.CompilerParams(vmem_limit_bytes=8 << 20),
        cost_estimate=pl.CostEstimate(flops=400_000_000, bytes_accessed=1 << 20, transcendentals=0),
        name="panel",
    )(
        in_hbm(query_grads.reshape(count, KG, KA)),
        in_hbm(ginv),
        in_hbm(ainv),
        in_hbm(lengths),
    )


def docs_kernel(first, lengths_ref, act_hbm, grad_hbm, *refs):
    out_ref, act_ref, grad_ref, sem = refs[-4:]
    owners = act_ref.shape[0]
    pitch = doc_pitch(owners)
    lane = lax.broadcasted_iota(jnp.int32, (1, 256), 1)

    def loads(o):
        tokens = pl.ds(pl.multiple_of((first + o) * TOK, TOK), TOK)
        return (
            pltpu.make_async_copy(act_hbm.at[0, :, tokens], act_ref.at[o], sem.at[0, o]),
            pltpu.make_async_copy(grad_hbm.at[0, :, tokens], grad_ref.at[o], sem.at[1, o]),
        )

    for o in range(owners):
        for load in loads(o):
            load.start()

    def owner(o, _):
        for load in loads(o):
            load.wait()
        row = first + o
        acts, grads = act_ref.at[o], grad_ref.at[o]

        def product(carry):
            j, start = carry
            base = pl.multiple_of(jnp.minimum(start >> 7, TOK // 128 - 2) * 128, 128)
            middle = start + lengths_ref[row, jnp.minimum(j, DOCS - 1)]
            end = middle + lengths_ref[row, jnp.minimum(j + 1, DOCS - 1)]
            window = grads[:, pl.ds(base, 256)]
            at = lane + base
            one = jnp.where((at >= start) & (at < middle), 1.0, 0.0).astype(BF16)
            two = jnp.where((at >= middle) & (at < end), 1.0, 0.0).astype(BF16)
            pair = lax.dot_general(
                jnp.concatenate([window * one, window * two], axis=0),
                acts[:, pl.ds(base, 256)],
                NT,
                preferred_element_type=F32,
            )
            out_ref[pl.ds(o * DOCS + j, KG, stride=pitch), :] = pair[:KG]
            out_ref[pl.ds(o * DOCS + j + 1, KG, stride=pitch), :] = pair[KG:]
            fits = end <= base + 256
            return (
                jnp.minimum(jnp.where(fits, j + 2, j + 1), DOCS),
                jnp.where(fits, end, middle),
            )

        carry = (jnp.int32(0), jnp.int32(0))
        for _ in range(STEPS):
            carry = product(carry)
        lax.while_loop(lambda c: c[0] < DOCS, lambda c: product(product(c)), carry)
        return 0

    lax.fori_loop(0, owners, owner, 0)


def doc_gradients(call, lengths, act_rows, grad_rows, after):
    owners = CALLS[call]
    return pl.pallas_call(
        functools.partial(docs_kernel, sum(CALLS[:call])),
        in_specs=[SMEM, HBM, HBM] + [ANY] * len(after),
        out_specs=VMEM,
        out_shape=pltpu.VMEM((KG * doc_pitch(owners), KA), F32),
        scratch_shapes=[
            pltpu.VMEM((owners, KA, TOK), BF16),
            pltpu.VMEM((owners, KG, TOK), BF16),
            pltpu.SemaphoreType.DMA((2, owners)),
        ],
        compiler_params=pltpu.CompilerParams(vmem_limit_bytes=14 << 20),
        cost_estimate=pl.CostEstimate(
            flops=owners * 2_000_000_000, bytes_accessed=owners * 5 << 19, transcendentals=0
        ),
        name="docs",
    )(lengths, in_hbm(act_rows), in_hbm(grad_rows), *after)


K_STEP = 1024


def group(pieces, after):
    flat = [part for piece in pieces for part in (piece if isinstance(piece, list) else [piece])]
    count = flat[0].shape[0]

    def kernel(*refs):
        out_ref, at = refs[-1], 0
        for ref in refs[len(after) : -1]:
            row, lane = divmod(at, WIDTH)
            out_ref[pl.ds(row * count, count), lane : lane + ref.shape[1]] = ref[...]
            at += ref.shape[1]

    return pl.pallas_call(
        kernel,
        in_specs=[VMEM] * (len(after) + len(flat)),
        out_specs=VMEM,
        out_shape=pltpu.VMEM((len(pieces) * count, WIDTH), BF16),
        compiler_params=pltpu.CompilerParams(vmem_limit_bytes=4 << 20),
        cost_estimate=pl.CostEstimate(flops=0, bytes_accessed=1 << 20, transcendentals=0),
        name="group",
    )(*map(in_vmem, after), *map(in_vmem, flat))


NEAR = (0, 2, 6, 8, 12)
FAR = (4, 10, 14)


def score_kernel(group_masks, blk_ref, *refs):
    *group_refs, out_ref, panels, total = refs
    docs_refs, group_refs = group_refs[: len(CALLS)], group_refs[len(CALLS) :]
    count = panels.shape[0] // 16
    for masks, group in zip(group_masks, group_refs):
        for i, m in enumerate(masks):
            panels[pl.ds(pl.multiple_of((blk_ref[0] ^ m) * count, count), count), :] = group[
                i * count : (i + 1) * count, :
            ]
    for k in range(0, WIDTH, K_STEP):
        documents = jnp.concatenate(
            [
                jnp.concatenate(
                    [
                        ref[pl.ds((k // KA + i) * doc_pitch(owners), owners * DOCS), :].astype(BF16)
                        for i in range(K_STEP // KA)
                    ],
                    axis=1,
                )
                for owners, ref in zip(CALLS, docs_refs)
            ],
            axis=0,
        )
        tile = lax.dot_general(documents, panels[:, k : k + K_STEP], NT, preferred_element_type=F32)
        if k == 0:
            total[...] = tile
        elif k < WIDTH - K_STEP:
            total[...] += tile
        else:
            out_ref[...] = (total[...] + tile).astype(BF16).reshape(out_ref.shape)


def partial_scores(blk, documents, group_masks, groups):
    count = sum(group.shape[0] for group in groups)
    return pl.pallas_call(
        functools.partial(score_kernel, group_masks),
        in_specs=[SMEM] + [VMEM] * (len(documents) + len(groups)),
        out_specs=VMEM,
        out_shape=pltpu.VMEM((OWNERS, DOCS, count), BF16),
        scratch_shapes=[
            pltpu.VMEM((count, WIDTH), BF16),
            pltpu.VMEM((OWNERS * DOCS, count), F32),
        ],
        compiler_params=pltpu.CompilerParams(vmem_limit_bytes=10 << 20),
        cost_estimate=pl.CostEstimate(
            flops=2 * OWNERS * DOCS * count * WIDTH, bytes_accessed=12 << 20, transcendentals=0
        ),
        name="scores",
    )(blk, *map(in_vmem, documents), *map(in_vmem, groups))


def local(act_rows, grad_rows, query_grads, ginv, ainv, lengths):
    blk = lax.axis_index("blk").astype(jnp.int32).reshape(1)

    def take(block, mask):
        return from_partner(block, "blk", mask)

    own, lengths = panel(query_grads, ginv, ainv, lengths)
    got = {0: own}
    for mask in NEAR[1:]:
        got[mask] = take(own, mask)

    lengths = lax.all_to_all(
        jnp.broadcast_to(lengths, (OWNERS, DOCS)), "tp", split_axis=0, concat_axis=0, tiled=True
    )

    near = group([got[m] for m in NEAR], [lengths])
    near_other = take(near, 1)
    count = own.shape[0]
    sent = {m: near[i * count : (i + 1) * count] for i, m in enumerate(NEAR)}
    got[4] = [take(sent[6][:, :HALF], 2), take(sent[2][:, HALF:], 6)]
    got[10], got[14] = take(sent[8], 2), take(sent[8], 6)
    low = doc_gradients(0, lengths, act_rows, grad_rows, [near_other])
    far = group([got[m] for m in FAR], [low])
    far_other = [take(far[i * count : (i + 1) * count], 1) for i in range(len(FAR))]
    high = doc_gradients(1, lengths, act_rows, grad_rows, [far])

    parts = partial_scores(
        blk,
        [low, high],
        [NEAR, FAR, [m ^ 1 for m in NEAR]] + [[m ^ 1] for m in FAR],
        [near, far, near_other, *far_other],
    )
    parts = lax.all_to_all(parts, "tp", split_axis=0, concat_axis=0)
    return jnp.sum(parts.astype(F32), axis=0)


def solution(mesh):
    placed = (
        P("tp", None, "blk"),
        P("tp", None, "blk"),
        P("blk", "tp", None, None),
        P("tp", None, None),
        P("tp", None, None),
        P(("blk", "tp"), None),
    )
    return jax.shard_map(
        local, mesh=mesh, in_specs=placed, out_specs=P(("blk", "tp"), None), check_vma=False
    )
```

```python
import functools

import jax
import jax.numpy as jnp
from jax import lax
from jax.experimental import pallas as pl
from jax.experimental.pallas import tpu as pltpu
from jax.sharding import PartitionSpec as P

F32, BF16 = jnp.float32, jnp.bfloat16
KA, KG, DOCS, TOK = 128, 64, 64, 4096
WIDTH = KA * KG
HALF = WIDTH // 2
NT = (((1,), (1,)), ((), ()))
OWNERS = 8
CALLS = (6, 2)
STEPS = 38
QUERY_PITCH = 24


def doc_pitch(owners):
    return owners * DOCS + 8


HBM = pl.BlockSpec(memory_space=pltpu.MemorySpace.HBM)
ANY = pl.BlockSpec(memory_space=pl.ANY)
VMEM = pl.BlockSpec(memory_space=pltpu.VMEM)
SMEM = pl.BlockSpec(memory_space=pltpu.SMEM)


def in_hbm(x):
    return pltpu.with_memory_space_constraint(x, pltpu.HBM)


def in_vmem(x):
    return pltpu.with_memory_space_constraint(x, pltpu.VMEM)


def from_partner(block, axis, mask):
    n = lax.axis_size(axis)
    return lax.ppermute(block, axis, [(i ^ mask, i) for i in range(n)])


def bf16_parts(x):
    first = x.astype(BF16)
    rest = x - first.astype(F32)
    second = rest.astype(BF16)
    third = (rest - second.astype(F32)).astype(BF16)
    return first, second, third


def panel_kernel(
    query_hbm, ginv_hbm, ainv_hbm, lengths_hbm,
    out_ref, lengths_ref,
    query_ref, ginv_ref, ainv_ref, rows, sem,
):
    count = query_ref.shape[0]
    loads = [
        pltpu.make_async_copy(ainv_hbm.at[0], ainv_ref, sem.at[0]),
        pltpu.make_async_copy(query_hbm, query_ref, sem.at[1]),
        pltpu.make_async_copy(ginv_hbm.at[0], ginv_ref, sem.at[2]),
        pltpu.make_async_copy(lengths_hbm, lengths_ref, sem.at[3]),
    ]
    for load in loads:
        load.start()
    for load in loads:
        load.wait()
    queries = query_ref[...].reshape(count * KG, KA)
    right = sum(
        jnp.dot(queries, part, preferred_element_type=F32)
        for part in reversed(bf16_parts(ainv_ref[...]))
    )
    side_by_side = jnp.concatenate(
        [right[q * KG : (q + 1) * KG] for q in range(count)], axis=1
    )
    both = jnp.dot(
        ginv_ref[...], side_by_side, precision=lax.Precision.HIGHEST, preferred_element_type=F32
    )
    for q in range(count):
        rows[pl.ds(q, KG, stride=QUERY_PITCH), :] = both[:, q * KA : (q + 1) * KA]
    for g in range(KG):
        out_ref[:, g * KA : (g + 1) * KA] = rows[pl.ds(g * QUERY_PITCH, count), :].astype(BF16)


def panel(query_grads, ginv, ainv, lengths):
    count = query_grads.shape[0]
    return pl.pallas_call(
        panel_kernel,
        in_specs=[HBM] * 4,
        out_specs=[VMEM, VMEM],
        out_shape=[pltpu.VMEM((count, WIDTH), BF16), pltpu.VMEM(lengths.shape, lengths.dtype)],
        scratch_shapes=[
            pltpu.VMEM((count, KG, KA), BF16),
            pltpu.VMEM((KG, KG), F32),
            pltpu.VMEM((KA, KA), F32),
            pltpu.VMEM(((KG + 1) * QUERY_PITCH, KA), F32),
            pltpu.SemaphoreType.DMA((4,)),
        ],
        compiler_params=pltpu.CompilerParams(vmem_limit_bytes=8 << 20),
        cost_estimate=pl.CostEstimate(flops=400_000_000, bytes_accessed=1 << 20, transcendentals=0),
        name="panel",
    )(
        in_hbm(query_grads.reshape(count, KG, KA)),
        in_hbm(ginv),
        in_hbm(ainv),
        in_hbm(lengths),
    )


def docs_kernel(first, lengths_ref, act_hbm, grad_hbm, *refs):
    out_ref, act_ref, grad_ref, sem = refs[-4:]
    owners = act_ref.shape[0]
    pitch = doc_pitch(owners)
    lane = lax.broadcasted_iota(jnp.int32, (1, 256), 1)

    def loads(o):
        tokens = pl.ds(pl.multiple_of((first + o) * TOK, TOK), TOK)
        return (
            pltpu.make_async_copy(act_hbm.at[0, :, tokens], act_ref.at[o], sem.at[0, o]),
            pltpu.make_async_copy(grad_hbm.at[0, :, tokens], grad_ref.at[o], sem.at[1, o]),
        )

    for o in range(owners):
        for load in loads(o):
            load.start()

    def owner(o, _):
        for load in loads(o):
            load.wait()
        row = first + o
        acts, grads = act_ref.at[o], grad_ref.at[o]

        def product(carry):
            j, start = carry
            base = pl.multiple_of(jnp.minimum(start >> 7, TOK // 128 - 2) * 128, 128)
            middle = start + lengths_ref[row, jnp.minimum(j, DOCS - 1)]
            end = middle + lengths_ref[row, jnp.minimum(j + 1, DOCS - 1)]
            window = grads[:, pl.ds(base, 256)]
            at = lane + base
            one = jnp.where((at >= start) & (at < middle), 1.0, 0.0).astype(BF16)
            two = jnp.where((at >= middle) & (at < end), 1.0, 0.0).astype(BF16)
            pair = lax.dot_general(
                jnp.concatenate([window * one, window * two], axis=0),
                acts[:, pl.ds(base, 256)],
                NT,
                preferred_element_type=F32,
            )
            out_ref[pl.ds(o * DOCS + j, KG, stride=pitch), :] = pair[:KG]
            out_ref[pl.ds(o * DOCS + j + 1, KG, stride=pitch), :] = pair[KG:]
            fits = end <= base + 256
            return (
                jnp.minimum(jnp.where(fits, j + 2, j + 1), DOCS),
                jnp.where(fits, end, middle),
            )

        carry = (jnp.int32(0), jnp.int32(0))
        for _ in range(STEPS):
            carry = product(carry)
        lax.while_loop(lambda c: c[0] < DOCS, lambda c: product(product(c)), carry)
        return 0

    lax.fori_loop(0, owners, owner, 0)


def doc_gradients(call, lengths, act_rows, grad_rows, after):
    owners = CALLS[call]
    return pl.pallas_call(
        functools.partial(docs_kernel, sum(CALLS[:call])),
        in_specs=[SMEM, HBM, HBM] + [ANY] * len(after),
        out_specs=VMEM,
        out_shape=pltpu.VMEM(((KG + 1) * doc_pitch(owners), KA), F32),
        scratch_shapes=[
            pltpu.VMEM((owners, KA, TOK), BF16),
            pltpu.VMEM((owners, KG, TOK), BF16),
            pltpu.SemaphoreType.DMA((2, owners)),
        ],
        compiler_params=pltpu.CompilerParams(vmem_limit_bytes=14 << 20),
        cost_estimate=pl.CostEstimate(
            flops=owners * 2_000_000_000, bytes_accessed=owners * 5 << 19, transcendentals=0
        ),
        name="docs",
    )(lengths, in_hbm(act_rows), in_hbm(grad_rows), *after)


K_STEP = 1024


def near_kernel(*refs):
    *piece_refs, near_ref, to2_ref, to6_ref = refs
    own, x2, x6, z, _ = piece_refs = piece_refs[-len(NEAR) :]
    count = own.shape[0]
    for i, ref in enumerate(piece_refs):
        near_ref[i * count : (i + 1) * count, :] = ref[...]
    to2_ref[:, :WIDTH] = z[...]
    to2_ref[:, WIDTH:] = x6[:, :HALF]
    to6_ref[:, :WIDTH] = z[...]
    to6_ref[:, WIDTH:] = x2[:, HALF:]


def far_kernel(*refs):
    from2, from6, far_ref = refs[-3:]
    count = from2.shape[0]
    far_ref[:count, :HALF] = from2[:, WIDTH:]
    far_ref[:count, HALF:] = from6[:, WIDTH:]
    far_ref[count : 2 * count, :] = from2[:, :WIDTH]
    far_ref[2 * count :, :] = from6[:, :WIDTH]


def regroup(kernel, shapes, pieces, after, name):
    return pl.pallas_call(
        kernel,
        in_specs=[VMEM] * (len(after) + len(pieces)),
        out_specs=[VMEM] * len(shapes),
        out_shape=[pltpu.VMEM(shape, BF16) for shape in shapes],
        compiler_params=pltpu.CompilerParams(vmem_limit_bytes=4 << 20),
        cost_estimate=pl.CostEstimate(flops=0, bytes_accessed=1 << 20, transcendentals=0),
        name=name,
    )(*map(in_vmem, after), *map(in_vmem, pieces))


NEAR = (0, 2, 6, 8, 12)
FAR = (4, 10, 14)


def score_kernel(group_masks, blk_ref, *refs):
    *group_refs, out_ref, panels, total = refs
    docs_refs, group_refs = group_refs[: len(CALLS)], group_refs[len(CALLS) :]
    count = panels.shape[0] // 16
    for masks, group in zip(group_masks, group_refs):
        for i, m in enumerate(masks):
            panels[pl.ds(pl.multiple_of((blk_ref[0] ^ m) * count, count), count), :] = group[
                i * count : (i + 1) * count, :
            ]
    for k in range(0, WIDTH, K_STEP):
        documents = jnp.concatenate(
            [
                jnp.concatenate(
                    [
                        ref[pl.ds((k // KA + i) * doc_pitch(owners), owners * DOCS), :].astype(BF16)
                        for i in range(K_STEP // KA)
                    ],
                    axis=1,
                )
                for owners, ref in zip(CALLS, docs_refs)
            ],
            axis=0,
        )
        tile = lax.dot_general(documents, panels[:, k : k + K_STEP], NT, preferred_element_type=F32)
        if k == 0:
            total[...] = tile
        elif k < WIDTH - K_STEP:
            total[...] += tile
        else:
            out_ref[...] = (total[...] + tile).astype(BF16).reshape(out_ref.shape)


def partial_scores(blk, documents, group_masks, groups):
    count = sum(group.shape[0] for group in groups)
    return pl.pallas_call(
        functools.partial(score_kernel, group_masks),
        in_specs=[SMEM] + [VMEM] * (len(documents) + len(groups)),
        out_specs=VMEM,
        out_shape=pltpu.VMEM((OWNERS, DOCS, count), BF16),
        scratch_shapes=[
            pltpu.VMEM((count, WIDTH), BF16),
            pltpu.VMEM((OWNERS * DOCS, count), F32),
        ],
        compiler_params=pltpu.CompilerParams(vmem_limit_bytes=10 << 20),
        cost_estimate=pl.CostEstimate(
            flops=2 * OWNERS * DOCS * count * WIDTH, bytes_accessed=12 << 20, transcendentals=0
        ),
        name="scores",
    )(blk, *map(in_vmem, documents), *map(in_vmem, groups))


def local(act_rows, grad_rows, query_grads, ginv, ainv, lengths):
    blk = lax.axis_index("blk").astype(jnp.int32).reshape(1)

    def take(block, mask):
        return from_partner(block, "blk", mask)

    own, lengths = panel(query_grads, ginv, ainv, lengths)
    got = {0: own}
    for mask in NEAR[1:]:
        got[mask] = take(own, mask)

    lengths = lax.all_to_all(
        jnp.broadcast_to(lengths, (OWNERS, DOCS)), "tp", split_axis=0, concat_axis=0, tiled=True
    )

    count = own.shape[0]
    near, to2, to6 = regroup(
        near_kernel,
        [(len(NEAR) * count, WIDTH)] + [(count, WIDTH + HALF)] * 2,
        [got[m] for m in NEAR],
        [lengths],
        "near",
    )
    near_other = take(near, 1)
    from2, from6 = take(to2, 2), take(to6, 6)
    low = doc_gradients(0, lengths, act_rows, grad_rows, [near_other])
    (far,) = regroup(far_kernel, [(len(FAR) * count, WIDTH)], [from2, from6], [low], "far")
    size = far.shape[0] // 3
    far_other = [take(far[i * size : (i + 1) * size], 1) for i in range(3)]
    high = doc_gradients(1, lengths, act_rows, grad_rows, [far])

    span = len(FAR) // 3
    parts = partial_scores(
        blk,
        [low, high],
        [NEAR, FAR, [m ^ 1 for m in NEAR]]
        + [[m ^ 1 for m in FAR[i * span : (i + 1) * span]] for i in range(3)],
        [near, far, near_other, *far_other],
    )
    parts = lax.all_to_all(parts, "tp", split_axis=0, concat_axis=0)
    return jnp.sum(parts.astype(F32), axis=0)


def solution(mesh):
    placed = (
        P("tp", None, "blk"),
        P("tp", None, "blk"),
        P("blk", "tp", None, None),
        P("tp", None, None),
        P("tp", None, None),
        P(("blk", "tp"), None),
    )
    return jax.shard_map(
        local, mesh=mesh, in_specs=placed, out_specs=P(("blk", "tp"), None), check_vma=False
    )
```

```python
import functools

import jax
import jax.numpy as jnp
from jax import lax
from jax.experimental import pallas as pl
from jax.experimental.pallas import tpu as pltpu
from jax.sharding import PartitionSpec as P

F32, BF16 = jnp.float32, jnp.bfloat16
KA, KG, DOCS, TOK = 128, 64, 64, 4096
WIDTH = KA * KG
HALF = WIDTH // 2
NT = (((1,), (1,)), ((), ()))
OWNERS = 8
CALLS = (6, 2)
STEPS = 38
QUERY_PITCH = 24


def doc_pitch(owners):
    return owners * DOCS + 8


HBM = pl.BlockSpec(memory_space=pltpu.MemorySpace.HBM)
ANY = pl.BlockSpec(memory_space=pl.ANY)
VMEM = pl.BlockSpec(memory_space=pltpu.VMEM)
SMEM = pl.BlockSpec(memory_space=pltpu.SMEM)


def in_hbm(x):
    return pltpu.with_memory_space_constraint(x, pltpu.HBM)


def in_vmem(x):
    return pltpu.with_memory_space_constraint(x, pltpu.VMEM)


def from_partner(block, axis, mask):
    n = lax.axis_size(axis)
    return lax.ppermute(block, axis, [(i ^ mask, i) for i in range(n)])


def bf16_parts(x):
    first = x.astype(BF16)
    rest = x - first.astype(F32)
    second = rest.astype(BF16)
    third = (rest - second.astype(F32)).astype(BF16)
    return first, second, third


def panel_kernel(
    query_hbm, ginv_hbm, ainv_hbm, lengths_hbm,
    out_ref, lengths_ref,
    query_ref, ginv_ref, ainv_ref, rows, sem,
):
    count = query_ref.shape[0]
    loads = [
        pltpu.make_async_copy(ainv_hbm.at[0], ainv_ref, sem.at[0]),
        pltpu.make_async_copy(query_hbm, query_ref, sem.at[1]),
        pltpu.make_async_copy(ginv_hbm.at[0], ginv_ref, sem.at[2]),
        pltpu.make_async_copy(lengths_hbm, lengths_ref, sem.at[3]),
    ]
    for load in loads:
        load.start()
    for load in loads:
        load.wait()
    queries = query_ref[...].reshape(count * KG, KA)
    right = sum(
        jnp.dot(queries, part, preferred_element_type=F32)
        for part in reversed(bf16_parts(ainv_ref[...]))
    )
    side_by_side = jnp.concatenate(
        [right[q * KG : (q + 1) * KG] for q in range(count)], axis=1
    )
    both = jnp.dot(
        ginv_ref[...], side_by_side, precision=lax.Precision.HIGHEST, preferred_element_type=F32
    )
    for q in range(count):
        rows[pl.ds(q, KG, stride=QUERY_PITCH), :] = both[:, q * KA : (q + 1) * KA]
    for g in range(KG):
        out_ref[:, g * KA : (g + 1) * KA] = rows[pl.ds(g * QUERY_PITCH, count), :].astype(BF16)


def panel(query_grads, ginv, ainv, lengths):
    count = query_grads.shape[0]
    return pl.pallas_call(
        panel_kernel,
        in_specs=[HBM] * 4,
        out_specs=[VMEM, VMEM],
        out_shape=[pltpu.VMEM((count, WIDTH), BF16), pltpu.VMEM(lengths.shape, lengths.dtype)],
        scratch_shapes=[
            pltpu.VMEM((count, KG, KA), BF16),
            pltpu.VMEM((KG, KG), F32),
            pltpu.VMEM((KA, KA), F32),
            pltpu.VMEM(((KG + 1) * QUERY_PITCH, KA), F32),
            pltpu.SemaphoreType.DMA((4,)),
        ],
        compiler_params=pltpu.CompilerParams(vmem_limit_bytes=8 << 20),
        cost_estimate=pl.CostEstimate(flops=400_000_000, bytes_accessed=1 << 20, transcendentals=0),
        name="panel",
    )(
        in_hbm(query_grads.reshape(count, KG, KA)),
        in_hbm(ginv),
        in_hbm(ainv),
        in_hbm(lengths),
    )


def docs_kernel(first, lengths_ref, act_hbm, grad_hbm, *refs):
    out_ref, act_ref, grad_ref, sem = refs[-4:]
    owners = act_ref.shape[0]
    pitch = doc_pitch(owners)
    lane = lax.broadcasted_iota(jnp.int32, (1, 256), 1)

    def loads(o):
        tokens = pl.ds(pl.multiple_of((first + o) * TOK, TOK), TOK)
        return (
            pltpu.make_async_copy(act_hbm.at[0, :, tokens], act_ref.at[o], sem.at[0, o]),
            pltpu.make_async_copy(grad_hbm.at[0, :, tokens], grad_ref.at[o], sem.at[1, o]),
        )

    for o in range(owners):
        for load in loads(o):
            load.start()

    def owner(o, _):
        for load in loads(o):
            load.wait()
        row = first + o
        acts, grads = act_ref.at[o], grad_ref.at[o]

        def product(carry):
            j, start = carry
            base = pl.multiple_of(jnp.minimum(start >> 7, TOK // 128 - 2) * 128, 128)
            middle = start + lengths_ref[row, jnp.minimum(j, DOCS - 1)]
            end = middle + lengths_ref[row, jnp.minimum(j + 1, DOCS - 1)]
            window = grads[:, pl.ds(base, 256)]
            at = lane + base
            one = jnp.where((at >= start) & (at < middle), 1.0, 0.0).astype(BF16)
            two = jnp.where((at >= middle) & (at < end), 1.0, 0.0).astype(BF16)
            pair = lax.dot_general(
                jnp.concatenate([window * one, window * two], axis=0),
                acts[:, pl.ds(base, 256)],
                NT,
                preferred_element_type=F32,
            )
            out_ref[pl.ds(o * DOCS + j, KG, stride=pitch), :] = pair[:KG]
            out_ref[pl.ds(o * DOCS + j + 1, KG, stride=pitch), :] = pair[KG:]
            fits = end <= base + 256
            return (
                jnp.minimum(jnp.where(fits, j + 2, j + 1), DOCS),
                jnp.where(fits, end, middle),
            )

        carry = (jnp.int32(0), jnp.int32(0))
        for _ in range(STEPS):
            carry = product(carry)
        lax.while_loop(lambda c: c[0] < DOCS, lambda c: product(product(c)), carry)
        return 0

    lax.fori_loop(0, owners, owner, 0)


def doc_gradients(call, lengths, act_rows, grad_rows, after):
    owners = CALLS[call]
    return pl.pallas_call(
        functools.partial(docs_kernel, sum(CALLS[:call])),
        in_specs=[SMEM, HBM, HBM] + [ANY] * len(after),
        out_specs=VMEM,
        out_shape=pltpu.VMEM(((KG + 1) * doc_pitch(owners), KA), F32),
        scratch_shapes=[
            pltpu.VMEM((owners, KA, TOK), BF16),
            pltpu.VMEM((owners, KG, TOK), BF16),
            pltpu.SemaphoreType.DMA((2, owners)),
        ],
        compiler_params=pltpu.CompilerParams(vmem_limit_bytes=14 << 20),
        cost_estimate=pl.CostEstimate(
            flops=owners * 2_000_000_000, bytes_accessed=owners * 5 << 19, transcendentals=0
        ),
        name="docs",
    )(lengths, in_hbm(act_rows), in_hbm(grad_rows), *after)


K_STEP = 1024


def near_kernel(*refs):
    *piece_refs, near_ref, to2_ref, to6_ref = refs
    own, x2, x6, z = piece_refs = piece_refs[-len(NEAR) :]
    count = own.shape[0]
    for i, ref in enumerate(piece_refs):
        near_ref[i * count : (i + 1) * count, :] = ref[...]
    to2_ref[:, :WIDTH] = z[...]
    to2_ref[:, WIDTH:] = x6[:, :HALF]
    to6_ref[:, :WIDTH] = z[...]
    to6_ref[:, WIDTH:] = x2[:, HALF:]


def far_kernel(*refs):
    from2, from6, whole, far_ref = refs[-4:]
    count = from2.shape[0]
    far_ref[:count, :HALF] = from2[:, WIDTH:]
    far_ref[:count, HALF:] = from6[:, WIDTH:]
    far_ref[count : 2 * count, :] = from2[:, :WIDTH]
    far_ref[2 * count : 3 * count, :] = from6[:, :WIDTH]
    far_ref[3 * count :, :] = whole[...]


def regroup(kernel, shapes, pieces, after, name):
    return pl.pallas_call(
        kernel,
        in_specs=[VMEM] * (len(after) + len(pieces)),
        out_specs=[VMEM] * len(shapes),
        out_shape=[pltpu.VMEM(shape, BF16) for shape in shapes],
        compiler_params=pltpu.CompilerParams(vmem_limit_bytes=4 << 20),
        cost_estimate=pl.CostEstimate(flops=0, bytes_accessed=1 << 20, transcendentals=0),
        name=name,
    )(*map(in_vmem, after), *map(in_vmem, pieces))


NEAR = (0, 2, 6, 8)
FAR = (4, 10, 14, 12)


def score_kernel(group_masks, blk_ref, *refs):
    *group_refs, out_ref, panels, total = refs
    docs_refs, group_refs = group_refs[: len(CALLS)], group_refs[len(CALLS) :]
    count = panels.shape[0] // 16
    for masks, group in zip(group_masks, group_refs):
        for i, m in enumerate(masks):
            panels[pl.ds(pl.multiple_of((blk_ref[0] ^ m) * count, count), count), :] = group[
                i * count : (i + 1) * count, :
            ]
    for k in range(0, WIDTH, K_STEP):
        documents = jnp.concatenate(
            [
                jnp.concatenate(
                    [
                        ref[pl.ds((k // KA + i) * doc_pitch(owners), owners * DOCS), :].astype(BF16)
                        for i in range(K_STEP // KA)
                    ],
                    axis=1,
                )
                for owners, ref in zip(CALLS, docs_refs)
            ],
            axis=0,
        )
        tile = lax.dot_general(documents, panels[:, k : k + K_STEP], NT, preferred_element_type=F32)
        if k == 0:
            total[...] = tile
        elif k < WIDTH - K_STEP:
            total[...] += tile
        else:
            out_ref[...] = (total[...] + tile).astype(BF16).reshape(out_ref.shape)


def partial_scores(blk, documents, group_masks, groups):
    count = sum(group.shape[0] for group in groups)
    return pl.pallas_call(
        functools.partial(score_kernel, group_masks),
        in_specs=[SMEM] + [VMEM] * (len(documents) + len(groups)),
        out_specs=VMEM,
        out_shape=pltpu.VMEM((OWNERS, DOCS, count), BF16),
        scratch_shapes=[
            pltpu.VMEM((count, WIDTH), BF16),
            pltpu.VMEM((OWNERS * DOCS, count), F32),
        ],
        compiler_params=pltpu.CompilerParams(vmem_limit_bytes=10 << 20),
        cost_estimate=pl.CostEstimate(
            flops=2 * OWNERS * DOCS * count * WIDTH, bytes_accessed=12 << 20, transcendentals=0
        ),
        name="scores",
    )(blk, *map(in_vmem, documents), *map(in_vmem, groups))


def local(act_rows, grad_rows, query_grads, ginv, ainv, lengths):
    blk = lax.axis_index("blk").astype(jnp.int32).reshape(1)

    def take(block, mask):
        return from_partner(block, "blk", mask)

    own, lengths = panel(query_grads, ginv, ainv, lengths)
    got = {0: own}
    for mask in (*NEAR[1:], 12):
        got[mask] = take(own, mask)

    lengths = lax.all_to_all(
        jnp.broadcast_to(lengths, (OWNERS, DOCS)), "tp", split_axis=0, concat_axis=0, tiled=True
    )

    count = own.shape[0]
    near, to2, to6 = regroup(
        near_kernel,
        [(len(NEAR) * count, WIDTH)] + [(count, WIDTH + HALF)] * 2,
        [got[m] for m in NEAR],
        [],
        "near",
    )
    near_other = take(near, 1)
    from2, from6 = take(to2, 2), take(to6, 6)
    low = doc_gradients(0, lengths, act_rows, grad_rows, [near])
    (far,) = regroup(far_kernel, [(len(FAR) * count, WIDTH)], [from2, from6, got[12]], [low], "far")
    size = far.shape[0] // 4
    far_other = [take(far[i * size : (i + 1) * size], 1) for i in range(4)]
    high = doc_gradients(1, lengths, act_rows, grad_rows, [far])

    span = len(FAR) // 4
    parts = partial_scores(
        blk,
        [low, high],
        [NEAR, FAR, [m ^ 1 for m in NEAR]]
        + [[m ^ 1 for m in FAR[i * span : (i + 1) * span]] for i in range(4)],
        [near, far, near_other, *far_other],
    )
    parts = lax.all_to_all(parts, "tp", split_axis=0, concat_axis=0)
    return jnp.sum(parts.astype(F32), axis=0)


def solution(mesh):
    placed = (
        P("tp", None, "blk"),
        P("tp", None, "blk"),
        P("blk", "tp", None, None),
        P("tp", None, None),
        P("tp", None, None),
        P(("blk", "tp"), None),
    )
    return jax.shard_map(
        local, mesh=mesh, in_specs=placed, out_specs=P(("blk", "tp"), None), check_vma=False
    )
```

```python
import functools

import jax
import jax.numpy as jnp
from jax import lax
from jax.experimental import pallas as pl
from jax.experimental.pallas import tpu as pltpu
from jax.sharding import PartitionSpec as P

F32, BF16 = jnp.float32, jnp.bfloat16
KA, KG, DOCS, TOK = 128, 64, 64, 4096
WIDTH = KA * KG
HALF = WIDTH // 2
NT = (((1,), (1,)), ((), ()))
OWNERS = 8
CALLS = (6, 2)
STEPS = 38
QUERY_PITCH = 24


def doc_pitch(owners):
    return owners * DOCS + 8


HBM = pl.BlockSpec(memory_space=pltpu.MemorySpace.HBM)
ANY = pl.BlockSpec(memory_space=pl.ANY)
VMEM = pl.BlockSpec(memory_space=pltpu.VMEM)
SMEM = pl.BlockSpec(memory_space=pltpu.SMEM)


def in_hbm(x):
    return pltpu.with_memory_space_constraint(x, pltpu.HBM)


def in_vmem(x):
    return pltpu.with_memory_space_constraint(x, pltpu.VMEM)


def from_partner(block, axis, mask):
    n = lax.axis_size(axis)
    return lax.ppermute(block, axis, [(i ^ mask, i) for i in range(n)])


def bf16_parts(x):
    first = x.astype(BF16)
    rest = x - first.astype(F32)
    second = rest.astype(BF16)
    third = (rest - second.astype(F32)).astype(BF16)
    return first, second, third


def panel_kernel(
    query_hbm, ginv_hbm, ainv_hbm, lengths_hbm,
    out_ref, copies_ref,
    query_ref, ginv_ref, ainv_ref, lengths_ref, rows, sem,
):
    count = query_ref.shape[0]
    loads = [
        pltpu.make_async_copy(ainv_hbm.at[0], ainv_ref, sem.at[0]),
        pltpu.make_async_copy(query_hbm, query_ref, sem.at[1]),
        pltpu.make_async_copy(ginv_hbm.at[0], ginv_ref, sem.at[2]),
        pltpu.make_async_copy(lengths_hbm, lengths_ref, sem.at[3]),
    ]
    for load in loads:
        load.start()
    for load in loads:
        load.wait()
    copies_ref[...] = jnp.broadcast_to(lengths_ref[...][None], copies_ref.shape)
    queries = query_ref[...].reshape(count * KG, KA)
    right = sum(
        jnp.dot(queries, part, preferred_element_type=F32)
        for part in reversed(bf16_parts(ainv_ref[...]))
    )
    side_by_side = jnp.concatenate(
        [right[q * KG : (q + 1) * KG] for q in range(count)], axis=1
    )
    both = jnp.dot(
        ginv_ref[...], side_by_side, precision=lax.Precision.HIGHEST, preferred_element_type=F32
    )
    for q in range(count):
        rows[pl.ds(q, KG, stride=QUERY_PITCH), :] = both[:, q * KA : (q + 1) * KA]
    for g in range(KG):
        out_ref[:, g * KA : (g + 1) * KA] = rows[pl.ds(g * QUERY_PITCH, count), :].astype(BF16)


def panel(query_grads, ginv, ainv, lengths):
    count = query_grads.shape[0]
    return pl.pallas_call(
        panel_kernel,
        in_specs=[HBM] * 4,
        out_specs=[VMEM, VMEM],
        out_shape=[pltpu.VMEM((count, WIDTH), BF16), pltpu.VMEM((OWNERS, *lengths.shape), lengths.dtype)],
        scratch_shapes=[
            pltpu.VMEM((count, KG, KA), BF16),
            pltpu.VMEM((KG, KG), F32),
            pltpu.VMEM((KA, KA), F32),
            pltpu.VMEM(lengths.shape, lengths.dtype),
            pltpu.VMEM(((KG + 1) * QUERY_PITCH, KA), F32),
            pltpu.SemaphoreType.DMA((4,)),
        ],
        compiler_params=pltpu.CompilerParams(vmem_limit_bytes=8 << 20),
        cost_estimate=pl.CostEstimate(flops=400_000_000, bytes_accessed=1 << 20, transcendentals=0),
        name="panel",
    )(
        in_hbm(query_grads.reshape(count, KG, KA)),
        in_hbm(ginv),
        in_hbm(ainv),
        in_hbm(lengths),
    )


def docs_kernel(first, lengths_ref, act_hbm, grad_hbm, *refs):
    out_ref, act_ref, grad_ref, sem = refs[-4:]
    owners = act_ref.shape[0]
    pitch = doc_pitch(owners)
    lane = lax.broadcasted_iota(jnp.int32, (1, 256), 1)

    def loads(o):
        tokens = pl.ds(pl.multiple_of((first + o) * TOK, TOK), TOK)
        return (
            pltpu.make_async_copy(act_hbm.at[0, :, tokens], act_ref.at[o], sem.at[0, o]),
            pltpu.make_async_copy(grad_hbm.at[0, :, tokens], grad_ref.at[o], sem.at[1, o]),
        )

    for o in range(owners):
        for load in loads(o):
            load.start()

    def owner(o, _):
        for load in loads(o):
            load.wait()
        row = first + o
        acts, grads = act_ref.at[o], grad_ref.at[o]

        def product(carry):
            j, start = carry
            base = pl.multiple_of(jnp.minimum(start >> 7, TOK // 128 - 2) * 128, 128)
            middle = start + lengths_ref[row, jnp.minimum(j, DOCS - 1)]
            end = middle + lengths_ref[row, jnp.minimum(j + 1, DOCS - 1)]
            window = grads[:, pl.ds(base, 256)]
            at = lane + base
            one = jnp.where((at >= start) & (at < middle), 1.0, 0.0).astype(BF16)
            two = jnp.where((at >= middle) & (at < end), 1.0, 0.0).astype(BF16)
            pair = lax.dot_general(
                jnp.concatenate([window * one, window * two], axis=0),
                acts[:, pl.ds(base, 256)],
                NT,
                preferred_element_type=F32,
            )
            out_ref[pl.ds(o * DOCS + j, KG, stride=pitch), :] = pair[:KG]
            out_ref[pl.ds(o * DOCS + j + 1, KG, stride=pitch), :] = pair[KG:]
            fits = end <= base + 256
            return (
                jnp.minimum(jnp.where(fits, j + 2, j + 1), DOCS),
                jnp.where(fits, end, middle),
            )

        carry = (jnp.int32(0), jnp.int32(0))
        for _ in range(STEPS):
            carry = product(carry)
        lax.while_loop(lambda c: c[0] < DOCS, lambda c: product(product(c)), carry)
        return 0

    lax.fori_loop(0, owners, owner, 0)


def doc_gradients(call, lengths, act_rows, grad_rows, after):
    owners = CALLS[call]
    return pl.pallas_call(
        functools.partial(docs_kernel, sum(CALLS[:call])),
        in_specs=[SMEM, HBM, HBM] + [ANY] * len(after),
        out_specs=VMEM,
        out_shape=pltpu.VMEM(((KG + 1) * doc_pitch(owners), KA), F32),
        scratch_shapes=[
            pltpu.VMEM((owners, KA, TOK), BF16),
            pltpu.VMEM((owners, KG, TOK), BF16),
            pltpu.SemaphoreType.DMA((2, owners)),
        ],
        compiler_params=pltpu.CompilerParams(vmem_limit_bytes=14 << 20),
        cost_estimate=pl.CostEstimate(
            flops=owners * 2_000_000_000, bytes_accessed=owners * 5 << 19, transcendentals=0
        ),
        name="docs",
    )(lengths, in_hbm(act_rows), in_hbm(grad_rows), *after)


K_STEP = 1024


def near_kernel(*refs):
    *piece_refs, near_ref, to2_ref, to6_ref = refs
    own, x2, x6, z = piece_refs = piece_refs[-len(NEAR) :]
    count = own.shape[0]
    for i, ref in enumerate(piece_refs):
        near_ref[i * count : (i + 1) * count, :] = ref[...]
    to2_ref[:, :WIDTH] = z[...]
    to2_ref[:, WIDTH:] = x6[:, :HALF]
    to6_ref[:, :WIDTH] = z[...]
    to6_ref[:, WIDTH:] = x2[:, HALF:]


def far_kernel(*refs):
    from2, from6, whole, far_ref = refs[-4:]
    count = from2.shape[0]
    far_ref[:count, :HALF] = from2[:, WIDTH:]
    far_ref[:count, HALF:] = from6[:, WIDTH:]
    far_ref[count : 2 * count, :] = from2[:, :WIDTH]
    far_ref[2 * count : 3 * count, :] = from6[:, :WIDTH]
    far_ref[3 * count :, :] = whole[...]


def regroup(kernel, shapes, pieces, after, name):
    return pl.pallas_call(
        kernel,
        in_specs=[VMEM] * (len(after) + len(pieces)),
        out_specs=[VMEM] * len(shapes),
        out_shape=[pltpu.VMEM(shape, BF16) for shape in shapes],
        compiler_params=pltpu.CompilerParams(vmem_limit_bytes=4 << 20),
        cost_estimate=pl.CostEstimate(flops=0, bytes_accessed=1 << 20, transcendentals=0),
        name=name,
    )(*map(in_vmem, after), *map(in_vmem, pieces))


NEAR = (0, 2, 6, 8)
FAR = (4, 10, 14, 12)


def score_kernel(group_masks, blk_ref, *refs):
    *group_refs, out_ref, panels, total = refs
    docs_refs, group_refs = group_refs[: len(CALLS)], group_refs[len(CALLS) :]
    count = panels.shape[0] // 16
    for masks, group in zip(group_masks, group_refs):
        for i, m in enumerate(masks):
            panels[pl.ds(pl.multiple_of((blk_ref[0] ^ m) * count, count), count), :] = group[
                i * count : (i + 1) * count, :
            ]
    for k in range(0, WIDTH, K_STEP):
        documents = jnp.concatenate(
            [
                jnp.concatenate(
                    [
                        ref[pl.ds((k // KA + i) * doc_pitch(owners), owners * DOCS), :].astype(BF16)
                        for i in range(K_STEP // KA)
                    ],
                    axis=1,
                )
                for owners, ref in zip(CALLS, docs_refs)
            ],
            axis=0,
        )
        tile = lax.dot_general(documents, panels[:, k : k + K_STEP], NT, preferred_element_type=F32)
        if k == 0:
            total[...] = tile
        elif k < WIDTH - K_STEP:
            total[...] += tile
        else:
            out_ref[...] = (total[...] + tile).astype(BF16).reshape(out_ref.shape)


def partial_scores(blk, documents, group_masks, groups):
    count = sum(group.shape[0] for group in groups)
    return pl.pallas_call(
        functools.partial(score_kernel, group_masks),
        in_specs=[SMEM] + [VMEM] * (len(documents) + len(groups)),
        out_specs=VMEM,
        out_shape=pltpu.VMEM((OWNERS, DOCS, count), BF16),
        scratch_shapes=[
            pltpu.VMEM((count, WIDTH), BF16),
            pltpu.VMEM((OWNERS * DOCS, count), F32),
        ],
        compiler_params=pltpu.CompilerParams(vmem_limit_bytes=10 << 20),
        cost_estimate=pl.CostEstimate(
            flops=2 * OWNERS * DOCS * count * WIDTH, bytes_accessed=12 << 20, transcendentals=0
        ),
        name="scores",
    )(blk, *map(in_vmem, documents), *map(in_vmem, groups))


def local(act_rows, grad_rows, query_grads, ginv, ainv, lengths):
    blk = lax.axis_index("blk").astype(jnp.int32).reshape(1)

    def take(block, mask):
        return from_partner(block, "blk", mask)

    own, lengths = panel(query_grads, ginv, ainv, lengths)
    got = {0: own}
    for mask in (*NEAR[1:], 12):
        got[mask] = take(own, mask)

    lengths = lax.all_to_all(lengths, "tp", split_axis=0, concat_axis=0, tiled=True)
    lengths = lengths.reshape(OWNERS, DOCS)

    count = own.shape[0]
    near, to2, to6 = regroup(
        near_kernel,
        [(len(NEAR) * count, WIDTH)] + [(count, WIDTH + HALF)] * 2,
        [got[m] for m in NEAR],
        [],
        "near",
    )
    near_other = take(near, 1)
    from2, from6 = take(to2, 2), take(to6, 6)
    low = doc_gradients(0, lengths, act_rows, grad_rows, [near])
    (far,) = regroup(far_kernel, [(len(FAR) * count, WIDTH)], [from2, from6, got[12]], [low], "far")
    size = far.shape[0] // 4
    far_other = [take(far[i * size : (i + 1) * size], 1) for i in range(4)]
    high = doc_gradients(1, lengths, act_rows, grad_rows, [far])

    span = len(FAR) // 4
    parts = partial_scores(
        blk,
        [low, high],
        [NEAR, FAR, [m ^ 1 for m in NEAR]]
        + [[m ^ 1 for m in FAR[i * span : (i + 1) * span]] for i in range(4)],
        [near, far, near_other, *far_other],
    )
    parts = lax.all_to_all(parts, "tp", split_axis=0, concat_axis=0)
    return jnp.sum(parts.astype(F32), axis=0)


def solution(mesh):
    placed = (
        P("tp", None, "blk"),
        P("tp", None, "blk"),
        P("blk", "tp", None, None),
        P("tp", None, None),
        P("tp", None, None),
        P(("blk", "tp"), None),
    )
    return jax.shard_map(
        local, mesh=mesh, in_specs=placed, out_specs=P(("blk", "tp"), None), check_vma=False
    )
```
